128 devices in a mesh: lat: 8 (over x, core), lon: 16 (over y, z).
Axes of the slice: x: 4, y: 4, z: 4, core: 2. Of those that a mesh axis runs over, the one named last changes fastest.
Arguments:
- tracers: float32 [10, 6, 128, 4096], P(None, None, 'lat', 'lon'), may hold values from 0.05 to 4
- forcing_groups: float32 [128, 128, 1728], P(('lat', 'lon')), as said below
- group_tiles: int32 [128, 128], P(('lat', 'lon')), may hold values from 0 to 127, each once within a row
- ocean_mask: int32 [128, 4096], P('lat', 'lon'), may hold values 0 or 1
- bio_rates: float32 [10, 10], replicated, may hold values from -2 to 2
- agent_traits: float32 [8, 16, 16, 64, 128], P('lat', 'lon'), may hold values from -6 to 6
- agent_cells: int32 [8, 16, 16, 128], P('lat'), may hold values from 0 to 4095
- agent_counts: int32 [8, 16, 16], P('lat'), may hold values from 0 to 128, as said below
- trait_weights: float32 [64, 64], replicated, may hold values from -0.75 to 0.75
- env_weights: float32 [60, 64], replicated, may hold values from -0.75 to 0.75
Outputs:
- tracers_out: float32 [10, 6, 128, 4096], P(None, None, 'lat', 'lon')
- agent_state: float32 [8, 16, 16, 64, 128], P('lat', 'lon')
The draws below stay inside these ranges and needn't reach their ends.
Inputs may be any that keep to these rules, and one draw needn't show every extreme that they name: `group_tiles`: each row lists every tile exactly once. `agent_counts`: live slots come first in each block; in every draw, all blocks bound for some one tile are full. `forcing_groups`: fields u and v lie in -0.2 to 0.2, kappa in 0.01 to 0.12.
All inputs are finite; a program needn't handle non-finite values. No bound on the sum of `ocean_mask` on one device may be relied on, other than what follows from the above.
Results may differ from the reference program's by a relative error of at most 0.0001.
Values sent between devices are 32-bit elements; how exact they have to be, the bound alone decides.
No kernel may reach another device: no remote copies, remote signals or barrier semaphores. Data moves between devices by JAX's collectives and lax.ppermute only.
A program may use at most 64 MiB of HBM per device.

```python
import math
import jax
import jax.numpy as jnp
from jax import lax

NTR = 10
TRAITS = 64
LEV = 6
SUBS = 3
CY = 16
CX = 256
SLOTS = 128
TILE_ROWS = 8
TILE_COLS = 16
TILES = 128
NY = 128
NX = 4096
BAND = 1728


def draw_forcing_groups(key, part):
    key_one, key_two = jax.random.split(key)
    shape = (TILES, TILES, BAND)
    reader = lax.broadcasted_iota(jnp.int32, shape, 0)
    position = lax.broadcasted_iota(jnp.int32, shape, 2)
    flat_index = reader * BAND + position
    field_index = flat_index // (LEV * CY * CX) % 3
    courant = jax.random.uniform(key_one, shape, jnp.float32, -0.2, 0.2)
    mixing = 0.01 * jnp.exp(jax.random.uniform(key_two, shape, jnp.float32) * jnp.log(12.0))
    return jnp.where(field_index == 2, mixing, courant)


def draw_agent_counts(key, part):
    key_one, key_two, key_three = jax.random.split(key, 3)
    density = jax.random.randint(key_one, (TILE_ROWS, 1, TILE_COLS), 1, 9)
    ceiling = jnp.minimum(SLOTS, SLOTS * density // 4)
    uniform_ints = jax.random.randint(key_two, (TILE_ROWS, TILE_COLS, TILE_COLS), 0, 65536)
    counts = uniform_ints * (ceiling + 1) // 65536
    full_tile = jax.random.randint(key_three, (), 0, TILE_ROWS * TILE_COLS)
    row_index = lax.broadcasted_iota(jnp.int32, counts.shape, 0)
    dest_index = lax.broadcasted_iota(jnp.int32, counts.shape, 2)
    chosen = row_index * TILE_COLS + dest_index == full_tile
    return jnp.where(chosen, SLOTS, counts).astype(jnp.int32)


def place_ends(result, key, least, largest):
    shape = result.shape
    index_at = [jax.random.randint(jax.random.fold_in(key, axis), (), 0, shape[axis]) for axis in range(len(shape))]
    result = result.at[tuple(index_at)].set(least)
    longest = shape.index(max(shape))
    index_at[longest] = (index_at[longest] + 1) % shape[longest]
    return result.at[tuple(index_at)].set(largest)


def block_levels(own_key, extent, cuts, least, high):
    gain = 1.0
    for dim, parts in cuts:
        heights = jax.random.uniform(jax.random.fold_in(jax.random.fold_in(own_key, 6), dim), (parts,), jnp.float32, least / len(cuts), high / len(cuts))
        gain = gain * jnp.repeat(jnp.exp(heights), extent[dim] // parts).reshape((-1,) + (1,) * (len(extent) - 1 - dim))
    return gain


def scatter_about(own_key, extent, width, most, cuts=(), kind=jnp.bfloat16):
    factor_of = block_levels(own_key, extent, cuts, -0.22, 0.18) if cuts else 1.0
    drawn = jax.random.normal(own_key, extent, jnp.float32) * width * factor_of
    return jnp.minimum(jnp.maximum(drawn, -most), most).astype(kind)


def setup_inputs(seed: int = 0) -> dict:
    key_list = jax.random.split(jax.random.key(seed), 11)
    return {
        "tracers": jnp.clip(jnp.exp(math.log(4.0) - 4.3820266 * jax.random.uniform(key_list[0], (NTR, LEV, NY, NX), jnp.float32) ** block_levels(key_list[0], (NTR, LEV, NY, NX), ((2, 8), (3, 16)), -0.2, 0.2)), 0.05, 4.0),
        "forcing_groups": draw_forcing_groups(jax.random.fold_in(key_list[10], 71), 0),
        "group_tiles": jax.vmap(lambda own: jax.random.permutation(own, TILES))(jax.random.split(key_list[2], TILES)).reshape((TILES, TILES)).astype(jnp.int32),
        "ocean_mask": place_ends((jax.random.randint(key_list[3], (NY, NX), 0, 4) < 3).astype(jnp.int32), jax.random.fold_in(key_list[3], 1), 0, 1),
        "bio_rates": scatter_about(key_list[4], (NTR, NTR), NTR ** -0.5, 2.0, (), jnp.float32),
        "agent_traits": scatter_about(key_list[5], (TILE_ROWS, TILE_COLS, TILE_COLS, TRAITS, SLOTS), 1.0, 6.0, ((0, 8), (1, 16)), jnp.float32),
        "agent_cells": place_ends(jax.random.randint(key_list[6], (TILE_ROWS, TILE_COLS, TILE_COLS, SLOTS), 0, CY * CX), jax.random.fold_in(key_list[6], 1), 0, (CY * CX) - 1).astype(jnp.int32),
        "agent_counts": draw_agent_counts(jax.random.fold_in(key_list[10], 71), 0),
        "trait_weights": scatter_about(key_list[8], (TRAITS, TRAITS), TRAITS ** -0.5, 0.75, (), jnp.float32),
        "env_weights": scatter_about(key_list[9], (NTR * LEV, TRAITS), (NTR * LEV) ** -0.5, 0.75, (), jnp.float32),
    }


PRECISE = lax.Precision.HIGHEST
BIO_STEP = 0.2


def advance(tracer_p, flow_east, flow_north, mixing, ocean_p, bio_rates):
    open_east = ocean_p[:, :-1] * ocean_p[:, 1:]
    speed_east = flow_east[:, :, :-1]
    flux_east = open_east * (jnp.maximum(speed_east, 0.0) * tracer_p[..., :-1] + jnp.minimum(speed_east, 0.0) * tracer_p[..., 1:])
    open_north = ocean_p[:-1, :] * ocean_p[1:, :]
    speed_north = flow_north[:, :-1, :]
    flux_north = open_north * (jnp.maximum(speed_north, 0.0) * tracer_p[..., :-1, :] + jnp.minimum(speed_north, 0.0) * tracer_p[..., 1:, :])
    center = tracer_p[..., 1:-1, 1:-1]
    spread = flux_east[..., 1:-1, 1:] - flux_east[..., 1:-1, :-1] + flux_north[..., 1:, 1:-1] - flux_north[..., :-1, 1:-1]
    kappa_lev = mixing[:-1, 1:-1, 1:-1]
    downward = kappa_lev * (center[:, 1:] - center[:, :-1])
    bottom_zero = jnp.zeros_like(downward[:, :1])
    vertical = jnp.concatenate([downward, bottom_zero], axis=1) - jnp.concatenate([bottom_zero, downward], axis=1)
    growth = jnp.einsum("ab,blyx->alyx", bio_rates, center, precision=PRECISE)
    return center + ocean_p[1:-1, 1:-1] * (vertical - spread + BIO_STEP * growth)


def pad_grid(grid_field):
    widths = [(0, 0)] * (grid_field.ndim - 2) + [(1, 1), (0, 0)]
    with_rows = jnp.pad(grid_field, widths)
    return jnp.concatenate([with_rows[..., -1:], with_rows, with_rows[..., :1]], axis=-1)


def one_tile(tile_env, tile_cells):
    return jnp.take(tile_env, tile_cells, axis=1)


def reference(tracers, forcing_groups, group_tiles, ocean_mask, bio_rates, agent_traits, agent_cells, agent_counts, trait_weights, env_weights):
    readers = jnp.arange(TILES, dtype=jnp.int32)[:, None]
    tile_bands = jnp.zeros_like(forcing_groups).at[group_tiles, readers].set(forcing_groups)
    forcing = tile_bands.reshape(TILE_ROWS, TILE_COLS, SUBS, 3, LEV, CY, CX).transpose(2, 3, 4, 0, 5, 1, 6).reshape(SUBS, 3, LEV, NY, NX)
    ocean_cells = pad_grid(ocean_mask.astype(jnp.float32))
    tracer_state = tracers
    for substep in range(SUBS):
        fields = pad_grid(forcing[substep])
        tracer_state = advance(pad_grid(tracer_state), fields[0], fields[1], fields[2], ocean_cells, bio_rates)
    arrived_traits = agent_traits.transpose(0, 2, 1, 3, 4)
    slot_cells = agent_cells.transpose(0, 2, 1, 3)
    live_counts = agent_counts.transpose(0, 2, 1)
    column_env = tracer_state.reshape(NTR * LEV, TILE_ROWS, CY, TILE_COLS, CX).transpose(1, 3, 0, 2, 4).reshape(TILE_ROWS, TILE_COLS, NTR * LEV, CY * CX)
    picked = jax.vmap(jax.vmap(one_tile))(column_env, slot_cells)
    activation = jnp.einsum("te,adnts->adnes", trait_weights, arrived_traits, precision=PRECISE) + jnp.einsum("ce,adcns->adnes", env_weights, picked, precision=PRECISE)
    alive_slots = (jnp.arange(SLOTS, dtype=jnp.int32)[None, None, None, :] < live_counts[..., None]).astype(jnp.float32)
    agent_state = alive_slots[:, :, :, None, :] * (arrived_traits + jnp.tanh(activation))
    return (tracer_state, agent_state)
```

```python
import jax
import jax.numpy as jnp
from jax import lax
from jax.experimental import pallas as pl
from jax.experimental.pallas import tpu as pltpu
from jax.sharding import PartitionSpec as P

NTR = 10
LEV = 6
SUBS = 3
CY = 16
CX = 256
BIO_STEP = 0.2

F32 = jnp.float32
BF16 = jnp.bfloat16

LINES = 14
BUSY = 10**12
FR = 26
NF = NTR * LEV + 1


def call(kernel, outs, scratch=(), limit=8, flops=0, in_specs=None, out_specs=None):
    return pl.pallas_call(
        kernel,
        out_shape=outs,
        scratch_shapes=list(scratch),
        **({"in_specs": in_specs} if in_specs else {}),
        **({"out_specs": out_specs} if out_specs else {}),
        compiler_params=pltpu.CompilerParams(vmem_limit_bytes=limit * 1024 * 1024),
        cost_estimate=pl.CostEstimate(flops=flops, bytes_accessed=0, transcendentals=0),
    )


def full(*shape, dtype=F32):
    return jax.ShapeDtypeStruct(shape, dtype)


def three_parts(x):
    hi = x.astype(BF16)
    rest = x - hi.astype(F32)
    mid = rest.astype(BF16)
    lo = (rest - mid.astype(F32)).astype(BF16)
    return hi, mid, lo


def dot(a, b):
    return jnp.dot(a, b, preferred_element_type=F32)


def lane_iota(rows=8):
    return lax.broadcasted_iota(jnp.int32, (rows, 128), 1)


def sort_bands_kernel(bands_ref, tiles_ref, out_ref, xs_ref):
    reader = lax.axis_index("lat") * 16 + lax.axis_index("lon")
    case = lax.rem(reader, 4)
    rows = 16
    for i in range(4):

        @pl.when(case == i)
        def _(i=i):
            spare = 0 if i % 2 else 64
            first = (0, 1, 1, 2)[i]
            lane = lane_iota(rows)
            pad = jnp.zeros((rows, 64), F32)
            for g in range(128 // rows):
                here = pl.ds(g * rows, rows)
                x = bands_ref[0, here, :]
                x = jnp.concatenate([pad, x] if i % 2 else [x, pad], axis=1)
                xs_ref[here, : LINES * 128] = x
                ends = jnp.zeros((rows, 128), F32)
                starts = jnp.zeros((rows, 128), F32)
                for j in range(7):
                    line = first + 2 * j
                    at = spare + 8 * j
                    if not (i == 3 and j == 6):
                        moved = x[:, line * 128 : line * 128 + 128]
                        if at:
                            moved = pltpu.roll(moved, at, 1)
                        starts = jnp.where((lane >= at) & (lane < at + 3), moved, starts)
                    if not (i == 0 and j == 0):
                        moved = x[:, line * 128 - 128 : line * 128]
                        if (at + 8) % 128:
                            moved = pltpu.roll(moved, at + 8, 1)
                        ends = jnp.where((lane >= at + 5) & (lane < at + 8), moved, ends)
                xs_ref[here, LINES * 128 : LINES * 128 + 128] = ends
                xs_ref[here, LINES * 128 + 128 :] = starts

    tiles = tiles_ref[0:1, :]
    me = lax.broadcasted_iota(jnp.int32, (128, 128), 0)
    west = (me & -16) | ((me - 1) & 15)
    east = (me & -16) | ((me + 1) & 15)
    one_hot = [(tiles == t).astype(F32).astype(BF16) for t in (me, west, east)]

    def pick(which, lo, hi):
        a, b, c = three_parts(xs_ref[:, lo:hi])
        m = one_hot[which]
        return (dot(m, c) + dot(m, b)) + dot(m, a)

    base = LINES * 128
    halo = pick(1, base, base + 128) + pick(2, base + 128, base + 256)
    odd = lax.rem(reader, 2) == 1
    for block in range(LINES // 2):
        t = pick(0, block * 256, block * 256 + 256)
        for k in range(2):
            line = 2 * block + k
            part = t[:, k * 128 : k * 128 + 128]
            if line == 0:
                part = part + jnp.where(odd, halo, 0.0)
            if line == LINES - 1:
                part = part + jnp.where(odd, 0.0, halo)
            for g in range(16):
                out_ref[pl.ds(8 * LINES * g + line, 8, stride=LINES), :] = part[8 * g : 8 * g + 8]


def north_rows():
    for s in range(2 + 1):
        for f in range(3):
            n = (2, 3, 2)[f] - s
            for l in range(LEV - (f == 2)):
                if n > 0:
                    yield s, f, l, n


def south_rows():
    for s in range(2):
        for f in range(3):
            for l in range(LEV - (f == 2)):
                yield s, f, l, 2 - s


NORTH = 3 * sum(r[3] for r in north_rows())
SOUTH = 3 * sum(r[3] for r in south_rows())


def unpack(lines_ref, flat_ref, edge_ref):
    lane = lane_iota()
    for p in range(64):
        a, b = 27 * p, 28 * p
        for to, frm in ((0, 0), (5, 5), (14, 15), (19, 20)):
            flat_ref[a + to : a + to + 8, :] = lines_ref[b + frm : b + frm + 8, :]
        flat_ref[a + 13 : a + 14, :] = jnp.where(
            lane[:1] < 64, lines_ref[b + 13 : b + 14, :], lines_ref[b + 14 : b + 15, :]
        )
    for gg in range(4):
        spare = [
            lines_ref[pl.ds(448 * gg + off, 8, stride=56), :] for off in (13, 14, 41, 42)
        ]
        for n in range(27):
            i, j = divmod(n, 7)
            right = pltpu.roll(spare[i], (128 - ((64, 0)[i % 2] + 8 * j)) % 128, 1)
            i, j = divmod(n + 1, 7)
            left = pltpu.roll(spare[i], (128 - ((64, 0)[i % 2] + 8 * j + 8)) % 128, 1)
            edge_ref[pl.ds(216 * gg + n, 8, stride=27), :] = jnp.where(lane < 64, right, left)


def edge_rows_kernel(lines_ref, west_ref, east_ref, north_ref, south_ref, flat_ref, edge_ref):
    unpack(lines_ref, flat_ref, edge_ref)
    at = 0
    for s, f, l, n in north_rows():
        q = (s * 3 + f) * LEV + l
        for h in range(2):
            north_ref[at : at + n, :] = flat_ref[pl.ds(32 * q + 2 * (CY - n) + h, n, stride=2), :]
            at += n
        north_ref[at : at + n, :] = edge_ref[16 * q + CY - n : 16 * q + CY, :]
        at += n
    at = 0
    for s, f, l, n in south_rows():
        q = (s * 3 + f) * LEV + l
        for h in range(2):
            south_ref[at : at + n, :] = flat_ref[pl.ds(32 * q + h, n, stride=2), :]
            at += n
        south_ref[at : at + n, :] = edge_ref[16 * q : 16 * q + n, :]
        at += n
    k = 0
    for ref in (west_ref, east_ref):
        for half in range(2):
            north_ref[NORTH + k : NORTH + k + 3, :] = ref[16 * half + 13 : 16 * half + 16, :]
            south_ref[SOUTH + k : SOUTH + k + 3, :] = ref[16 * half : 16 * half + 3, :]
            k += 3


def field(tracers_ref, ocean_ref, f, rows, cols):
    if f < NTR * LEV:
        l, c = divmod(f, NTR)
        return tracers_ref[c, l, rows, cols]
    return ocean_ref[rows, cols].astype(F32)


def ends_kernel(tracers_ref, ocean_ref, north_ref, south_ref, east_ref, west_ref):
    lane = lane_iota()
    for f in range(NF):
        for h in range(2):
            cols = slice(128 * h, 128 * h + 128)
            at = (f * 2 + h) * 3
            north_ref[at : at + 3, :] = field(tracers_ref, ocean_ref, f, slice(CY - 3, CY), cols)
            south_ref[at : at + 3, :] = field(tracers_ref, ocean_ref, f, slice(0, 3), cols)
    for half in range(2):
        for g in range(2):
            rows = slice(8 * g, 8 * g + 8)
            east = jnp.zeros((8, 128), F32)
            west = jnp.zeros((8, 128), F32)
            for f in range(32 * half, min(32 * half + 32, NF)):
                m = 4 * (f % 32)
                use = (lane >= m) & (lane < m + 3)
                last = field(tracers_ref, ocean_ref, f, rows, slice(128, 256))
                first = field(tracers_ref, ocean_ref, f, rows, slice(0, 128))
                east = jnp.where(use, pltpu.roll(last, (m + 3) % 128, 1), east)
                west = jnp.where(use, pltpu.roll(first, m, 1) if m else first, west)
            to = 16 * half + 8 * g
            east_ref[to : to + 8, :] = east
            west_ref[to : to + 8, :] = west


def fill_frames(
    tracers_ref, ocean_ref, below_ref, above_ref, west_ref, east_ref, f_below_ref, f_above_ref,
    main_ref, side_ref, ends_ref,
):
    zero = jnp.zeros((4, 128), F32)
    for f in range(NF):
        for h in range(2):
            cols = slice(128 * h, 128 * h + 128)
            at, frm = (f * 2 + h) * FR, (f * 2 + h) * 3
            main_ref[at : at + 3, :] = below_ref[frm : frm + 3, :]
            for g in range(2):
                main_ref[at + 3 + 8 * g : at + 11 + 8 * g, :] = field(
                    tracers_ref, ocean_ref, f, slice(8 * g, 8 * g + 8), cols
                )
            main_ref[at + 19 : at + 22, :] = above_ref[frm : frm + 3, :]
            main_ref[at + 22 : at + 26, :] = zero
    for k in range(4):
        ref, half, to = (west_ref, east_ref)[k // 2], k % 2, 24 * k
        ends_ref[to : to + 3, :] = f_below_ref[NORTH + 3 * k : NORTH + 3 * k + 3, :]
        ends_ref[to + 3 : to + 11, :] = ref[16 * half : 16 * half + 8, :]
        ends_ref[to + 11 : to + 19, :] = ref[16 * half + 8 : 16 * half + 16, :]
        ends_ref[to + 19 : to + 22, :] = f_above_ref[SOUTH + 3 * k : SOUTH + 3 * k + 3, :]
        ends_ref[to + 22 : to + 24, :] = zero[:2]
    lane = lane_iota()
    for f in range(NF):
        m = 4 * (f % 32)
        frm = 24 * (f // 32)
        for g in range(3):
            right = ends_ref[48 + frm + 8 * g : 56 + frm + 8 * g, :]
            if m:
                right = pltpu.roll(right, 128 - m, 1)
            left = pltpu.roll(ends_ref[frm + 8 * g : frm + 8 * g + 8, :], 125 - m, 1)
            side_ref[f * FR + 8 * g : f * FR + 8 * g + 8, :] = jnp.where(lane < 64, right, left)
        side_ref[f * FR + 24 : f * FR + 26, :] = zero[:2]


def shift_east(tiles, lane):
    moved = [pltpu.roll(t, 127, 1) for t in tiles]
    n = len(tiles)
    return [jnp.where(lane == 127, moved[(h + 1) % n], moved[h]) for h in range(n)]


def shift_west(tiles, lane):
    moved = [pltpu.roll(t, 1, 1) for t in tiles]
    n = len(tiles)
    return [jnp.where(lane == 0, moved[(h - 1) % n], moved[h]) for h in range(n)]


def transport_kernel(
    tracers_ref,
    ocean_ref,
    t_below_ref,
    t_above_ref,
    west_ref,
    east_ref,
    rates_ref,
    lines_ref,
    below_ref,
    above_ref,
    hot_hbm_ref,
    yrow_ref,
    out_ref,
    picked_ref,
    flat_ref,
    edge_ref,
    u_ref,
    v_ref,
    k_ref,
    main_ref,
    side_ref,
    ends_ref,
    main1_ref,
    side1_ref,
    main2_ref,
    side2_ref,
    coef_ref,
    env_ref,
    lhs_ref,
    hot_ref,
    hot_sem,
):
    hot_copy = pltpu.make_async_copy(hot_hbm_ref, hot_ref, hot_sem)
    hot_copy.start()
    fill_frames(
        tracers_ref, ocean_ref, t_below_ref, t_above_ref, west_ref, east_ref, below_ref, above_ref,
        main_ref, side_ref, ends_ref,
    )
    lane = lane_iota()
    unpack(lines_ref, flat_ref, edge_ref)

    below, above = {}, {}
    at = 0
    for s, f, l, n in north_rows():
        below[s, f, l] = (at, n)
        at += 3 * n
    at = 0
    for s, f, l, n in south_rows():
        above[s, f, l] = (at, n)
        at += 3 * n
    for s in range(SUBS):
        for f in range(3):
            ref = (u_ref, v_ref, k_ref)[f]
            for l in range(LEV - (f == 2)):
                q = (s * 3 + f) * LEV + l
                k = s * LEV + l if f < 2 else s * (LEV + 1) + l + 1
                for h in range(3):
                    to = (k * 3 + h) * FR
                    for g in range(2):
                        if h < 2:
                            part = flat_ref[pl.ds(32 * q + 16 * g + h, 8, stride=2), :]
                        else:
                            part = edge_ref[16 * q + 8 * g : 16 * q + 8 * g + 8, :]
                        ref[to + 3 + 8 * g : to + 11 + 8 * g, :] = part
                    if (s, f, l) in below:
                        frm, n = below[s, f, l]
                        ref[to + 3 - n : to + 3, :] = below_ref[frm + h * n : frm + h * n + n, :]
                    if (s, f, l) in above:
                        frm, n = above[s, f, l]
                        ref[to + 19 : to + 19 + n, :] = above_ref[frm + h * n : frm + h * n + n, :]
        for k in (s * (LEV + 1), s * (LEV + 1) + LEV):
            for r in range(0, 3 * FR, 6):
                k_ref[k * 3 * FR + r : k * 3 * FR + r + 6, :] = jnp.zeros((6, 128), F32)

    def substep(s, src, dst):
        start = 1 if s < 2 else 3
        groups = 3 if s < 2 else 2
        width = 3 if s < 2 else 2
        smain, sside = src

        def body(t, _):
            l = lax.div(t, groups)
            g = lax.rem(t, groups)
            row = start + 8 * g

            def frame(f, h, off=0):
                if h < 2:
                    return smain[pl.ds((f * 2 + h) * FR + row + off, 8), :]
                return sside[pl.ds(f * FR + row + off, 8), :]

            def forcing(ref, k, h, off=0):
                return ref[pl.ds((k * 3 + h) * FR + row + off, 8), :]

            def ocean(h, off=0):
                f = NTR * LEV
                if h < 2:
                    return main_ref[pl.ds((f * 2 + h) * FR + row + off, 8), :]
                return side_ref[pl.ds(f * FR + row + off, 8), :]

            o = [ocean(h) for h in range(3)]
            u = [forcing(u_ref, s * LEV + l, h) for h in range(3)]
            open_east = [a * b for a, b in zip(o, shift_east(o, lane))]
            up = [w * jnp.maximum(x, 0.0) for w, x in zip(open_east, u)]
            um = [w * jnp.minimum(x, 0.0) for w, x in zip(open_east, u)]
            up_w, um_w = shift_west(up, lane), shift_west(um, lane)
            for h in range(width):
                v = forcing(v_ref, s * LEV + l, h)
                v_s = forcing(v_ref, s * LEV + l, h, -1)
                open_n, open_s = o[h] * ocean(h, 1), o[h] * ocean(h, -1)
                vp, vm = open_n * jnp.maximum(v, 0.0), open_n * jnp.minimum(v, 0.0)
                vp_s, vm_s = open_s * jnp.maximum(v_s, 0.0), open_s * jnp.minimum(v_s, 0.0)
                k_up = o[h] * forcing(k_ref, s * (LEV + 1) + l + 1, h)
                k_dn = o[h] * forcing(k_ref, s * (LEV + 1) + l, h)
                own = (um_w[h] - up[h]) + (vm_s - vp) - (k_up + k_dn)
                own = own + 1.0
                values = (own, -um[h], up_w[h], -vm, vp_s, k_up, k_dn, o[h])
                for i, value in enumerate(values):
                    coef_ref[(h * 8 + i) * 8 : (h * 8 + i) * 8 + 8, :] = value

            def coef(h, i):
                return coef_ref[(h * 8 + i) * 8 : (h * 8 + i) * 8 + 8, :]

            l_up, l_dn = jnp.minimum(l + 1, LEV - 1), jnp.maximum(l - 1, 0)
            cells = [[frame(l * NTR + c, h) for h in range(3)] for c in range(NTR)]
            for a in range(NTR):
                f = l * NTR + a
                rate = rates_ref[a * NTR]
                grown = [rate * cells[0][h] for h in range(width)]
                for b in range(1, NTR):
                    rate = rates_ref[a * NTR + b]
                    grown = [grown[h] + rate * cells[b][h] for h in range(width)]
                east, west = shift_east(cells[a], lane), shift_west(cells[a], lane)
                for h in range(width):
                    value = coef(h, 0) * cells[a][h] + coef(h, 7) * grown[h]
                    value = value + coef(h, 1) * east[h] + coef(h, 2) * west[h]
                    value = value + coef(h, 3) * frame(f, h, 1) + coef(h, 4) * frame(f, h, -1)
                    value = value + coef(h, 5) * frame(l_up * NTR + a, h)
                    value = value + coef(h, 6) * frame(l_dn * NTR + a, h)
                    if s == 2:
                        rows = pl.ds(pl.multiple_of(8 * g, 8), 8)
                        out_ref[a, l, rows, 128 * h : 128 * h + 128] = value
                        env_ref[h, pl.ds((a * LEV + l) * CY + 8 * g, 8), :] = value
                    elif h < 2:
                        dst[0][pl.ds((f * 2 + h) * FR + row, 8), :] = value
                    else:
                        dst[1][pl.ds(f * FR + row, 8), :] = value
            return 0

        lax.fori_loop(0, groups * LEV, body, 0)

    substep(0, (main_ref, side_ref), (main1_ref, side1_ref))
    substep(1, (main1_ref, side1_ref), (main2_ref, side2_ref))
    substep(2, (main2_ref, side2_ref), None)

    env_ref[:, NTR * LEV * CY :, :] = jnp.zeros((2, 4 * CY, 128), F32)
    for y in range(CY):
        for h in range(2):
            part = [env_ref[h, pl.ds(128 * k + y, 8, stride=CY), :] for k in range(8)]
            x = jnp.concatenate(part, axis=0)
            hi = x.astype(BF16)
            lo = (x - hi.astype(F32)).astype(BF16)
            lhs_ref[128 * y : 128 * y + 64, 128 * h : 128 * h + 128] = hi
            lhs_ref[128 * y + 64 : 128 * y + 128, 128 * h : 128 * h + 128] = lo

    hot_copy.wait()

    def slots(n, _):
        cols = pl.ds(pl.multiple_of(256 * n, 256), 256)
        found = dot(lhs_ref[...], hot_ref[:, cols])
        row = yrow_ref[0:1, cols]
        total = jnp.where(row == 0, found[:128], 0.0)
        for y in range(1, CY):
            total = total + jnp.where(row == y, found[128 * y : 128 * y + 128], 0.0)
        picked_ref[:, cols] = total.astype(BF16)
        return 0

    lax.fori_loop(0, 8, slots, 0)


def slots_kernel(cells_ref, hot_ref, yrow_ref):
    own = lax.axis_index("lon")
    column = lax.broadcasted_iota(jnp.int32, (256, 128), 0)
    for n in range(16):
        cell = cells_ref[0, n, pl.ds(own, 1), :]
        hot_ref[:, 128 * n : 128 * n + 128] = ((cell & 255) == column).astype(F32).astype(BF16)
        yrow_ref[:, 128 * n : 128 * n + 128] = lax.shift_right_logical(cell, 8)


def agents_kernel(traits_ref, picked_ref, tw_ref, ew_ref, counts_ref, out_ref, weights_ref):
    own = lax.axis_index("lon")
    ew = jnp.concatenate([ew_ref[...], jnp.zeros((4, 64), F32)], axis=0)
    for k, w in enumerate((tw_ref[...], ew)):
        w = w.T
        hi = w.astype(BF16)
        lo = (w - hi.astype(F32)).astype(BF16)
        for i, part in enumerate((hi, hi, lo)):
            weights_ref[:, (3 * k + i) * 64 : (3 * k + i) * 64 + 64] = part
    slot = lax.broadcasted_iota(jnp.int32, (64, 128), 1)
    for n in range(0, 16, 2):
        x = jnp.concatenate([traits_ref[n], traits_ref[n + 1]], axis=1)
        hi = x.astype(BF16)
        lo = (x - hi.astype(F32)).astype(BF16)
        picked = picked_ref[:, 128 * n : 128 * n + 256]
        rhs = jnp.concatenate([hi, lo, hi, picked, picked[:64]], axis=0)
        new = x + jnp.tanh(dot(weights_ref[...], rhs))
        for k in range(2):
            live = slot < counts_ref[0, n + k, own]
            out_ref[n + k] = jnp.where(live, new[:, 128 * k : 128 * k + 128], 0.0)


def shards(
    tracers,
    forcing_groups,
    group_tiles,
    ocean_mask,
    bio_rates,
    agent_traits,
    agent_cells,
    agent_counts,
    trait_weights,
    env_weights,
):
    north = [(i, i + 1) for i in range(7)]
    south = [(i + 1, i) for i in range(7)]
    east = [(i, (i + 1) % 16) for i in range(16)]
    west = [((i + 1) % 16, i) for i in range(16)]

    vmem = pl.BlockSpec(memory_space=pltpu.VMEM)
    hbm = pl.BlockSpec(memory_space=pltpu.HBM)

    lines = call(
        sort_bands_kernel,
        full(128 * LINES, 128),
        [pltpu.VMEM((128, LINES * 128 + 256), F32)],
    )(forcing_groups, group_tiles)
    lines = lines.reshape(128, 1, LINES * 128)
    lines = lax.all_to_all(lines, ("lat", "lon"), split_axis=0, concat_axis=0, tiled=True)
    lines = lines.reshape(128 * LINES, 128)

    n_rows, n_cols = full(NF * 6, 128), full(32, 128)
    to_north, to_south, to_east, to_west = call(ends_kernel, (n_rows, n_rows, n_cols, n_cols))(
        tracers, ocean_mask
    )
    below = lax.ppermute(to_north, "lat", north)
    above = lax.ppermute(to_south, "lat", south)
    from_west = lax.ppermute(to_east, "lon", east)
    from_east = lax.ppermute(to_west, "lon", west)
    rates = jnp.broadcast_to((BIO_STEP * bio_rates).reshape(NTR * NTR, 1, 1), (NTR * NTR, 8, 128))
    hot, yrow = call(
        slots_kernel, (full(256, 2048, dtype=BF16), full(1, 2048, dtype=jnp.int32))
    )(agent_cells)
    lines, below, above, from_west, from_east, hot, yrow, rates = lax.optimization_barrier(
        (lines, below, above, from_west, from_east, hot, yrow, rates)
    )
    f_north, f_south = call(
        edge_rows_kernel,
        (full(NORTH + 12, 128), full(SOUTH + 12, 128)),
        [pltpu.VMEM((1728, 128), F32), pltpu.VMEM((864, 128), F32)],
    )(lines, from_west, from_east)
    f_below = lax.ppermute(f_north, "lat", north)
    f_above = lax.ppermute(f_south, "lat", south)
    traits, _ = lax.optimization_barrier((agent_traits[0, 0], f_north))
    received = lax.all_to_all(traits, "lon", split_axis=0, concat_axis=0, tiled=True)

    n_main, n_side = NTR * LEV * 2 * FR, NTR * LEV * FR
    tracers_out, picked = call(
        transport_kernel,
        (full(NTR, LEV, CY, CX), full(128, 2048, dtype=BF16)),
        [
            pltpu.VMEM((1728, 128), F32),
            pltpu.VMEM((864, 128), F32),
            pltpu.VMEM((SUBS * LEV * 3 * FR, 128), F32),
            pltpu.VMEM((SUBS * LEV * 3 * FR, 128), F32),
            pltpu.VMEM((SUBS * (LEV + 1) * 3 * FR, 128), F32),
            pltpu.VMEM((NF * 2 * FR, 128), F32),
            pltpu.VMEM((NF * FR, 128), F32),
            pltpu.VMEM((96, 128), F32),
            pltpu.VMEM((n_main, 128), F32),
            pltpu.VMEM((n_side, 128), F32),
            pltpu.VMEM((n_main, 128), F32),
            pltpu.VMEM((n_side, 128), F32),
            pltpu.VMEM((3 * 8 * 8, 128), F32),
            pltpu.VMEM((2, 64 * CY, 128), F32),
            pltpu.VMEM((128 * CY, 256), BF16),
            pltpu.VMEM((256, 2048), BF16),
            pltpu.SemaphoreType.DMA,
        ],
        limit=20,
        in_specs=[vmem] * 10 + [hbm, vmem],
        flops=BUSY,
    )(tracers, ocean_mask, below, above, from_west, from_east, rates, lines, f_below, f_above, pltpu.with_memory_space_constraint(hot, pltpu.HBM), yrow)

    agent_state = call(
        agents_kernel,
        full(16, 64, 128),
        [pltpu.VMEM((64, 384), BF16)],
        in_specs=[vmem] * 4 + [pl.BlockSpec(memory_space=pltpu.SMEM)],
    )(received, picked, trait_weights, env_weights, agent_counts)
    return (tracers_out, agent_state[None, None])


def solution(mesh):
    placed = (
        P(None, None, "lat", "lon"),
        P(("lat", "lon"), None, None),
        P(("lat", "lon"), None),
        P("lat", "lon"),
        P(),
        P("lat", "lon", None, None, None),
        P("lat", None, None, None),
        P("lat", None, None),
        P(),
        P(),
    )
    return jax.shard_map(
        shards,
        mesh=mesh,
        in_specs=placed,
        out_specs=(P(None, None, "lat", "lon"), P("lat", "lon", None, None, None)),
        check_vma=False,
    )
```

```python
import jax
import jax.numpy as jnp
from jax import lax
from jax.experimental import pallas as pl
from jax.experimental.pallas import tpu as pltpu
from jax.sharding import PartitionSpec as P

NTR = 10
LEV = 6
SUBS = 3
CY = 16
CX = 256
BIO_STEP = 0.2
PRECISE = lax.Precision.HIGHEST

F32 = jnp.float32
BF16 = jnp.bfloat16

LINES = 14
PITCH = 65
BUSY = 10**12
FR = 26
NF = NTR * LEV + 1


def call(kernel, outs, scratch=(), limit=8, flops=0, in_specs=None, out_specs=None):
    return pl.pallas_call(
        kernel,
        out_shape=outs,
        scratch_shapes=list(scratch),
        **({"in_specs": in_specs} if in_specs else {}),
        **({"out_specs": out_specs} if out_specs else {}),
        compiler_params=pltpu.CompilerParams(vmem_limit_bytes=limit * 1024 * 1024),
        cost_estimate=pl.CostEstimate(flops=flops, bytes_accessed=0, transcendentals=0),
    )


def full(*shape, dtype=F32):
    return jax.ShapeDtypeStruct(shape, dtype)


def three_parts(x):
    hi = x.astype(BF16)
    rest = x - hi.astype(F32)
    mid = rest.astype(BF16)
    lo = (rest - mid.astype(F32)).astype(BF16)
    return hi, mid, lo


def dot(a, b):
    return jnp.dot(a, b, preferred_element_type=F32)


def lane_iota(rows=8):
    return lax.broadcasted_iota(jnp.int32, (rows, 128), 1)


def sort_bands_kernel(bands_hbm_ref, tiles_hbm_ref, out_ref, xs_ref, ends_ref, tiles_ref, in_sems):
    reader = lax.axis_index("lat") * 16 + lax.axis_index("lon")
    odd = lax.rem(reader, 2)
    top = pl.multiple_of(8 + 64 * odd, 8)
    chunk = 432
    copies = [
        pltpu.make_async_copy(
            bands_hbm_ref.at[0, pl.ds(chunk * k, chunk)],
            xs_ref.at[pl.ds(pl.multiple_of(top + chunk * k, 8), chunk)],
            in_sems.at[k],
        )
        for k in range(4)
    ]
    tiles_copy = pltpu.make_async_copy(tiles_hbm_ref, tiles_ref, in_sems.at[4])
    tiles_copy.start()
    for copy in copies:
        copy.start()
    spare = pl.multiple_of(64 * (1 - odd), 8)
    xs_ref[0:8, :] = jnp.zeros((8, 128), F32)
    xs_ref[8 + LINES * 128 : 16 + LINES * 128, :] = jnp.zeros((8, 128), F32)
    xs_ref[pl.ds(pl.multiple_of(8 + 27 * 64 * (1 - odd), 8), 64), :] = jnp.zeros((64, 128), F32)
    ends_ref[...] = jnp.zeros(ends_ref.shape, F32)

    tiles_copy.wait()
    tiles = tiles_ref[0:1, :]
    me = lax.broadcasted_iota(jnp.int32, (128, 128), 0)
    west = (me & -16) | ((me - 1) & 15)
    east = (me & -16) | ((me + 1) & 15)
    own_hot, west_hot, east_hot = [
        (tiles == t).astype(F32).astype(BF16) for t in (me, west, east)
    ]

    def pick(hot, k_rows):
        a, b, c = [
            lax.dot_general(hot, part, (((1,), (1,)), ((), ())), preferred_element_type=F32)
            for part in k_rows
        ]
        return (c + b) + a

    def sort_block(block, halo):
        lo = 8 + 256 * block
        t = pick(own_hot, three_parts(xs_ref[lo : lo + 256, :]))
        for k in range(2):
            line = 2 * block + k
            part = t[:, k * 128 : k * 128 + 128]
            if line == 0:
                part = part + jnp.where(odd == 1, halo, 0.0)
            if line == LINES - 1:
                part = part + jnp.where(odd == 1, 0.0, halo)
            for g in range(16):
                out_ref[pl.ds(8 * LINES * g + line, 8, stride=LINES), :] = part[8 * g : 8 * g + 8]

    arrived = 0
    for block in range(1, LINES // 2 - 1):
        while arrived * chunk < 256 * block + 256:
            copies[arrived].wait()
            arrived += 1
        sort_block(block, None)
    case = lax.rem(reader, 4)
    first = lax.div(case + 1, 2)
    for j in range(7):
        at = 8 + 128 * first + 256 * j
        ends_ref[pl.ds(spare + 8 * j + 5, 3), :] = xs_ref[pl.ds(at - 3, 3), :]
        ends_ref[pl.ds(128 + spare + 8 * j, 3), :] = xs_ref[pl.ds(at, 3), :]
    parts = three_parts(ends_ref[...])
    halo = pick(west_hot, [p[:128] for p in parts]) + pick(east_hot, [p[128:] for p in parts])
    sort_block(0, halo)
    sort_block(LINES // 2 - 1, halo)


def north_rows():
    for s in range(2 + 1):
        for f in range(3):
            n = (2, 3, 2)[f] - s
            for l in range(LEV - (f == 2)):
                if n > 0:
                    yield s, f, l, n


def south_rows():
    for s in range(2):
        for f in range(3):
            for l in range(LEV - (f == 2)):
                yield s, f, l, 2 - s


NORTH = 3 * sum(r[3] for r in north_rows())
SOUTH = 3 * sum(r[3] for r in south_rows())


def unpack(lines_ref, flat_ref, edge_ref):
    lane = lane_iota()
    for p in range(64):
        a, b = 27 * p, 28 * p
        for to, frm in ((0, 0), (5, 5), (14, 15), (19, 20)):
            flat_ref[a + to : a + to + 8, :] = lines_ref[b + frm : b + frm + 8, :]
        flat_ref[a + 13 : a + 14, :] = jnp.where(
            lane[:1] < 64, lines_ref[b + 13 : b + 14, :], lines_ref[b + 14 : b + 15, :]
        )
    for gg in range(4):
        spare = [
            lines_ref[pl.ds(448 * gg + off, 8, stride=56), :] for off in (13, 14, 41, 42)
        ]
        for n in range(27):
            i, j = divmod(n, 7)
            right = pltpu.roll(spare[i], (128 - ((64, 0)[i % 2] + 8 * j)) % 128, 1)
            i, j = divmod(n + 1, 7)
            left = pltpu.roll(spare[i], (128 - ((64, 0)[i % 2] + 8 * j + 8)) % 128, 1)
            edge_ref[pl.ds(216 * gg + n, 8, stride=27), :] = jnp.where(lane < 64, right, left)


def edge_rows_kernel(lines_ref, west_ref, east_ref, north_ref, south_ref, flat_ref, edge_ref):
    unpack(lines_ref, flat_ref, edge_ref)
    at = 0
    for s, f, l, n in north_rows():
        q = (s * 3 + f) * LEV + l
        for h in range(2):
            north_ref[at : at + n, :] = flat_ref[pl.ds(32 * q + 2 * (CY - n) + h, n, stride=2), :]
            at += n
        north_ref[at : at + n, :] = edge_ref[16 * q + CY - n : 16 * q + CY, :]
        at += n
    at = 0
    for s, f, l, n in south_rows():
        q = (s * 3 + f) * LEV + l
        for h in range(2):
            south_ref[at : at + n, :] = flat_ref[pl.ds(32 * q + h, n, stride=2), :]
            at += n
        south_ref[at : at + n, :] = edge_ref[16 * q : 16 * q + n, :]
        at += n
    k = 0
    for ref in (west_ref, east_ref):
        for half in range(2):
            north_ref[NORTH + k : NORTH + k + 3, :] = ref[16 * half + 13 : 16 * half + 16, :]
            south_ref[SOUTH + k : SOUTH + k + 3, :] = ref[16 * half : 16 * half + 3, :]
            k += 3


def field(tracers_ref, ocean_ref, f, rows, cols):
    if f < NTR * LEV:
        l, c = divmod(f, NTR)
        return tracers_ref[c, l, rows, cols]
    return ocean_ref[rows, cols].astype(F32)


def ends_kernel(tracers_ref, ocean_ref, north_ref, south_ref, east_ref, west_ref):
    lane = lane_iota()
    for f in range(NF):
        for h in range(2):
            cols = slice(128 * h, 128 * h + 128)
            at = (f * 2 + h) * 3
            north_ref[at : at + 3, :] = field(tracers_ref, ocean_ref, f, slice(CY - 3, CY), cols)
            south_ref[at : at + 3, :] = field(tracers_ref, ocean_ref, f, slice(0, 3), cols)
    for half in range(2):
        for g in range(2):
            rows = slice(8 * g, 8 * g + 8)
            east = jnp.zeros((8, 128), F32)
            west = jnp.zeros((8, 128), F32)
            for f in range(32 * half, min(32 * half + 32, NF)):
                m = 4 * (f % 32)
                use = (lane >= m) & (lane < m + 3)
                last = field(tracers_ref, ocean_ref, f, rows, slice(128, 256))
                first = field(tracers_ref, ocean_ref, f, rows, slice(0, 128))
                east = jnp.where(use, pltpu.roll(last, (m + 3) % 128, 1), east)
                west = jnp.where(use, pltpu.roll(first, m, 1) if m else first, west)
            to = 16 * half + 8 * g
            east_ref[to : to + 8, :] = east
            west_ref[to : to + 8, :] = west


def fill_frames(
    tracers_ref, ocean_ref, below_ref, above_ref, west_ref, east_ref, f_below_ref, f_above_ref,
    main_ref, side_ref, ends_ref,
):
    zero = jnp.zeros((4, 128), F32)
    for f in range(NF):
        for h in range(2):
            cols = slice(128 * h, 128 * h + 128)
            at, frm = (f * 2 + h) * FR, (f * 2 + h) * 3
            main_ref[at : at + 3, :] = below_ref[frm : frm + 3, :]
            for g in range(2):
                main_ref[at + 3 + 8 * g : at + 11 + 8 * g, :] = field(
                    tracers_ref, ocean_ref, f, slice(8 * g, 8 * g + 8), cols
                )
            main_ref[at + 19 : at + 22, :] = above_ref[frm : frm + 3, :]
            main_ref[at + 22 : at + 26, :] = zero
    for k in range(4):
        ref, half, to = (west_ref, east_ref)[k // 2], k % 2, 24 * k
        ends_ref[to : to + 3, :] = f_below_ref[NORTH + 3 * k : NORTH + 3 * k + 3, :]
        ends_ref[to + 3 : to + 11, :] = ref[16 * half : 16 * half + 8, :]
        ends_ref[to + 11 : to + 19, :] = ref[16 * half + 8 : 16 * half + 16, :]
        ends_ref[to + 19 : to + 22, :] = f_above_ref[SOUTH + 3 * k : SOUTH + 3 * k + 3, :]
        ends_ref[to + 22 : to + 24, :] = zero[:2]
    lane = lane_iota()
    for f in range(NF):
        m = 4 * (f % 32)
        frm = 24 * (f // 32)
        for g in range(3):
            right = ends_ref[48 + frm + 8 * g : 56 + frm + 8 * g, :]
            if m:
                right = pltpu.roll(right, 128 - m, 1)
            left = pltpu.roll(ends_ref[frm + 8 * g : frm + 8 * g + 8, :], 125 - m, 1)
            side_ref[f * FR + 8 * g : f * FR + 8 * g + 8, :] = jnp.where(lane < 64, right, left)
        side_ref[f * FR + 24 : f * FR + 26, :] = zero[:2]


def shift_east(tiles, lane):
    moved = [pltpu.roll(t, 127, 1) for t in tiles]
    n = len(tiles)
    return [jnp.where(lane == 127, moved[(h + 1) % n], moved[h]) for h in range(n)]


def shift_west(tiles, lane):
    moved = [pltpu.roll(t, 1, 1) for t in tiles]
    n = len(tiles)
    return [jnp.where(lane == 0, moved[(h - 1) % n], moved[h]) for h in range(n)]


def transport_kernel(
    tracers_ref,
    ocean_ref,
    t_below_ref,
    t_above_ref,
    west_ref,
    east_ref,
    bio_ref,
    lines_ref,
    below_ref,
    above_ref,
    hot_hbm_ref,
    yrow_ref,
    out_hbm_ref,
    picked_ref,
    flat_ref,
    edge_ref,
    u_ref,
    v_ref,
    k_ref,
    main_ref,
    side_ref,
    ends_ref,
    main1_ref,
    side1_ref,
    main2_ref,
    side2_ref,
    env_ref,
    lhs_ref,
    hot_ref,
    rates_ref,
    out_ref,
    sems,
    *work_refs,
):
    hot_copy = pltpu.make_async_copy(hot_hbm_ref, hot_ref, sems.at[0])
    hot_copy.start()

    shape = (8 * NTR, NTR)
    spread = lax.broadcasted_iota(jnp.int32, shape, 0) // 8 == lax.broadcasted_iota(jnp.int32, shape, 1)
    spread = spread.astype(F32)
    wide = jnp.dot(spread, BIO_STEP * bio_ref[...], preferred_element_type=F32, precision=PRECISE)
    wide = lax.dot_general(
        wide, spread, (((1,), (1,)), ((), ())), preferred_element_type=F32, precision=PRECISE
    )
    row = lax.broadcasted_iota(jnp.int32, wide.shape, 0)
    column = lax.broadcasted_iota(jnp.int32, wide.shape, 1)
    wide = jnp.where((row & 7) == (column & 7), wide, 0.0)
    hi = wide.astype(BF16)
    lo = (wide - hi.astype(F32)).astype(BF16)
    rates_ref[...] = jnp.concatenate([hi, hi, lo], axis=1)
    fill_frames(
        tracers_ref, ocean_ref, t_below_ref, t_above_ref, west_ref, east_ref, below_ref, above_ref,
        main_ref, side_ref, ends_ref,
    )
    lane = lane_iota()
    unpack(lines_ref, flat_ref, edge_ref)

    below, above = {}, {}
    at = 0
    for s, f, l, n in north_rows():
        below[s, f, l] = (at, n)
        at += 3 * n
    at = 0
    for s, f, l, n in south_rows():
        above[s, f, l] = (at, n)
        at += 3 * n
    for s in range(SUBS):
        for f in range(3):
            ref = (u_ref, v_ref, k_ref)[f]
            for l in range(LEV - (f == 2)):
                q = (s * 3 + f) * LEV + l
                k = s * LEV + l if f < 2 else s * (LEV + 1) + l + 1
                for h in range(3):
                    to = (k * 3 + h) * FR
                    if s == 0:
                        ref[to + 19 : to + 26, :] = jnp.zeros((7, 128), F32)
                    for g in range(2):
                        if h < 2:
                            part = flat_ref[pl.ds(32 * q + 16 * g + h, 8, stride=2), :]
                        else:
                            part = edge_ref[16 * q + 8 * g : 16 * q + 8 * g + 8, :]
                        ref[to + 3 + 8 * g : to + 11 + 8 * g, :] = part
                    if (s, f, l) in below:
                        frm, n = below[s, f, l]
                        ref[to + 3 - n : to + 3, :] = below_ref[frm + h * n : frm + h * n + n, :]
                    if (s, f, l) in above:
                        frm, n = above[s, f, l]
                        ref[to + 19 : to + 19 + n, :] = above_ref[frm + h * n : frm + h * n + n, :]
        for k in (s * (LEV + 1), s * (LEV + 1) + LEV):
            for r in range(0, 3 * FR, 6):
                k_ref[k * 3 * FR + r : k * 3 * FR + r + 6, :] = jnp.zeros((6, 128), F32)

    def substep(s, src, dst):
        start = 1 if s < 2 else 3
        groups = 3 if s < 2 else 2
        width = 3 if s < 2 else 2
        smain, sside = src

        def place(t):
            l = lax.div(t, groups)
            g = lax.rem(t, groups)
            return l, g, start + 8 * g

        def readers(row):
            def frame(f, h, off=0):
                if h < 2:
                    return smain[pl.ds((f * 2 + h) * FR + row + off, 8), :]
                return sside[pl.ds(f * FR + row + off, 8), :]

            def forcing(ref, k, h, off=0):
                return ref[pl.ds((k * 3 + h) * FR + row + off, 8), :]

            def ocean(h, off=0):
                f = NTR * LEV
                if h < 2:
                    return main_ref[pl.ds((f * 2 + h) * FR + row + off, 8), :]
                return side_ref[pl.ds(f * FR + row + off, 8), :]

            return frame, forcing, ocean

        def prepare(t, slot):
            split_ref, grown_ref, coef_ref = work_refs[3 * slot : 3 * slot + 3]
            l, g, row = place(t)
            frame, forcing, ocean = readers(row)
            for h in range(width):
                x = jnp.concatenate([frame(l * NTR + c, h) for c in range(NTR)], axis=0)
                hi = x.astype(BF16)
                lo = (x - hi.astype(F32)).astype(BF16)
                cols = slice(128 * h, 128 * h + 128)
                split_ref[0:80, cols] = hi
                split_ref[80:160, cols] = lo
                split_ref[160:240, cols] = hi
            grown_ref[:, : 128 * width] = dot(rates_ref[...], split_ref[:, : 128 * width])

            o = [ocean(h) for h in range(3)]
            u = [forcing(u_ref, s * LEV + l, h) for h in range(3)]
            open_east = [a * b for a, b in zip(o, shift_east(o, lane))]
            up = [w * jnp.maximum(x, 0.0) for w, x in zip(open_east, u)]
            um = [w * jnp.minimum(x, 0.0) for w, x in zip(open_east, u)]
            up_w, um_w = shift_west(up, lane), shift_west(um, lane)
            for h in range(width):
                v = forcing(v_ref, s * LEV + l, h)
                v_s = forcing(v_ref, s * LEV + l, h, -1)
                open_n, open_s = o[h] * ocean(h, 1), o[h] * ocean(h, -1)
                vp, vm = open_n * jnp.maximum(v, 0.0), open_n * jnp.minimum(v, 0.0)
                vp_s, vm_s = open_s * jnp.maximum(v_s, 0.0), open_s * jnp.minimum(v_s, 0.0)
                k_up = o[h] * forcing(k_ref, s * (LEV + 1) + l + 1, h)
                k_dn = o[h] * forcing(k_ref, s * (LEV + 1) + l, h)
                own = (um_w[h] - up[h]) + (vm_s - vp) - (k_up + k_dn)
                own = own + 1.0
                values = (own, -um[h], up_w[h], -vm, vp_s, k_up, k_dn, o[h])
                for i, value in enumerate(values):
                    coef_ref[(h * 8 + i) * 8 : (h * 8 + i) * 8 + 8, :] = value

        def transport(t, slot):
            grown_ref, coef_ref = work_refs[3 * slot + 1 : 3 * slot + 3]
            l, g, row = place(t)
            frame = readers(row)[0]

            l_up, l_dn = jnp.minimum(l + 1, LEV - 1), jnp.maximum(l - 1, 0)
            coefs = [
                [coef_ref[(h * 8 + i) * 8 : (h * 8 + i) * 8 + 8, :] for i in range(8)]
                for h in range(width)
            ]
            for a in range(NTR):
                f = l * NTR + a
                cell = [frame(f, h) for h in range(3)]
                east, west = shift_east(cell, lane), shift_west(cell, lane)
                for h in range(width):
                    own, k_e, k_w, k_n, k_s, k_up, k_dn, water = coefs[h]
                    value = (own * cell[h] + k_e * east[h]) + (k_w * west[h] + k_n * frame(f, h, 1))
                    value = value + (k_s * frame(f, h, -1) + k_up * frame(l_up * NTR + a, h))
                    value = value + k_dn * frame(l_dn * NTR + a, h)
                    value = value + water * grown_ref[8 * a : 8 * a + 8, 128 * h : 128 * h + 128]
                    if s == 2:
                        rows = pl.ds(pl.multiple_of(8 * g, 8), 8)
                        out_ref[a, l, rows, 128 * h : 128 * h + 128] = value
                        env_ref[h, pl.ds(8 * PITCH * g + a * LEV + l, 8, stride=PITCH), :] = value
                    elif h < 2:
                        dst[0][pl.ds((f * 2 + h) * FR + row, 8), :] = value
                    else:
                        dst[1][pl.ds(f * FR + row, 8), :] = value

        count = groups * LEV

        def body(k, _):
            prepare(2 * k + 1, 1)
            transport(2 * k, 0)
            prepare(jnp.minimum(2 * k + 2, count - 1), 0)
            transport(2 * k + 1, 1)
            return 0

        prepare(0, 0)
        lax.fori_loop(0, count // 2, body, 0)

    substep(0, (main_ref, side_ref), (main1_ref, side1_ref))
    substep(1, (main1_ref, side1_ref), (main2_ref, side2_ref))
    substep(2, (main2_ref, side2_ref), None)

    out_copy = pltpu.make_async_copy(out_ref, out_hbm_ref, sems.at[1])
    out_copy.start()

    for y in range(CY):
        for h in range(2):
            env_ref[h, PITCH * y + NTR * LEV : PITCH * y + 64, :] = jnp.zeros((4, 128), F32)
            x = env_ref[h, PITCH * y : PITCH * y + 64, :]
            hi = x.astype(BF16)
            lo = (x - hi.astype(F32)).astype(BF16)
            lhs_ref[128 * y : 128 * y + 64, 128 * h : 128 * h + 128] = hi
            lhs_ref[128 * y + 64 : 128 * y + 128, 128 * h : 128 * h + 128] = lo

    hot_copy.wait()

    def slots(n, _):
        cols = pl.ds(pl.multiple_of(256 * n, 256), 256)
        found = dot(lhs_ref[...], hot_ref[:, cols])
        row = yrow_ref[0:1, cols]
        total = jnp.where(row == 0, found[:64] + found[64:128], 0.0)
        for y in range(1, CY):
            here = found[128 * y : 128 * y + 64] + found[128 * y + 64 : 128 * y + 128]
            total = total + jnp.where(row == y, here, 0.0)
        hi = total.astype(BF16)
        picked_ref[0:64, cols] = hi
        picked_ref[64:128, cols] = (total - hi.astype(F32)).astype(BF16)
        return 0

    lax.fori_loop(0, 8, slots, 0)
    out_copy.wait()


def slots_kernel(cells_ref, hot_ref, yrow_ref):
    own = lax.axis_index("lon")
    column = lax.broadcasted_iota(jnp.int32, (256, 128), 0)
    for n in range(16):
        cell = cells_ref[0, n, pl.ds(own, 1), :]
        hot_ref[:, 128 * n : 128 * n + 128] = ((cell & 255) == column).astype(F32).astype(BF16)
        yrow_ref[:, 128 * n : 128 * n + 128] = lax.shift_right_logical(cell, 8)


def agents_kernel(traits_ref, picked_ref, tw_ref, ew_ref, counts_ref, out_ref, weights_ref):
    own = lax.axis_index("lon")
    ew = jnp.concatenate([ew_ref[...], jnp.zeros((4, 64), F32)], axis=0)
    for k, w in enumerate((tw_ref[...], ew)):
        w = w.T
        hi = w.astype(BF16)
        lo = (w - hi.astype(F32)).astype(BF16)
        for i, part in enumerate((hi, hi, lo)):
            weights_ref[:, (3 * k + i) * 64 : (3 * k + i) * 64 + 64] = part
    slot = lax.broadcasted_iota(jnp.int32, (64, 128), 1)
    for n in range(0, 16, 2):
        x = jnp.concatenate([traits_ref[n], traits_ref[n + 1]], axis=1)
        hi = x.astype(BF16)
        lo = (x - hi.astype(F32)).astype(BF16)
        picked = picked_ref[:, 128 * n : 128 * n + 256]
        rhs = jnp.concatenate([hi, lo, hi, picked, picked[:64]], axis=0)
        new = x + jnp.tanh(dot(weights_ref[...], rhs))
        for k in range(2):
            live = slot < counts_ref[0, n + k, own]
            out_ref[n + k] = jnp.where(live, new[:, 128 * k : 128 * k + 128], 0.0)


def shards(
    tracers,
    forcing_groups,
    group_tiles,
    ocean_mask,
    bio_rates,
    agent_traits,
    agent_cells,
    agent_counts,
    trait_weights,
    env_weights,
):
    north = [(i, i + 1) for i in range(7)]
    south = [(i + 1, i) for i in range(7)]
    east = [(i, (i + 1) % 16) for i in range(16)]
    west = [((i + 1) % 16, i) for i in range(16)]

    vmem = pl.BlockSpec(memory_space=pltpu.VMEM)
    hbm = pl.BlockSpec(memory_space=pltpu.HBM)

    bands = jnp.swapaxes(forcing_groups, 1, 2)
    lines = call(
        sort_bands_kernel,
        pltpu.VMEM((128 * LINES, 128), F32),
        [
            pltpu.VMEM((16 + LINES * 128, 128), F32),
            pltpu.VMEM((256, 128), F32),
            pltpu.VMEM((1, 128), jnp.int32),
            pltpu.SemaphoreType.DMA((5,)),
        ],
        in_specs=[hbm, hbm],
    )(
        pltpu.with_memory_space_constraint(bands, pltpu.HBM),
        pltpu.with_memory_space_constraint(group_tiles, pltpu.HBM),
    )
    lines = lines.reshape(128, 1, LINES * 128)
    lines = lax.all_to_all(lines, ("lat", "lon"), split_axis=0, concat_axis=0, tiled=True)
    lines = lines.reshape(128 * LINES, 128)

    n_rows, n_cols = full(NF * 6, 128), full(32, 128)
    to_north, to_south, to_east, to_west = call(ends_kernel, (n_rows, n_rows, n_cols, n_cols))(
        tracers, ocean_mask
    )
    below = lax.ppermute(to_north, "lat", north)
    above = lax.ppermute(to_south, "lat", south)
    from_west = lax.ppermute(to_east, "lon", east)
    from_east = lax.ppermute(to_west, "lon", west)
    hot, yrow = call(
        slots_kernel, (full(256, 2048, dtype=BF16), full(1, 2048, dtype=jnp.int32))
    )(agent_cells)
    lines, below, above, from_west, from_east, hot, yrow = lax.optimization_barrier(
        (lines, below, above, from_west, from_east, hot, yrow)
    )
    f_north, f_south = call(
        edge_rows_kernel,
        (full(NORTH + 12, 128), full(SOUTH + 12, 128)),
        [pltpu.VMEM((1728, 128), F32), pltpu.VMEM((864, 128), F32)],
    )(lines, from_west, from_east)
    f_below = lax.ppermute(f_north, "lat", north)
    f_above = lax.ppermute(f_south, "lat", south)
    traits, _ = lax.optimization_barrier((agent_traits[0, 0], f_north))
    received = lax.all_to_all(traits, "lon", split_axis=0, concat_axis=0, tiled=True)

    n_main, n_side = NTR * LEV * 2 * FR, NTR * LEV * FR
    tracers_out, picked = call(
        transport_kernel,
        (pltpu.HBM((NTR, LEV, CY, CX), F32), full(128, 2048, dtype=BF16)),
        [
            pltpu.VMEM((1728, 128), F32),
            pltpu.VMEM((864, 128), F32),
            pltpu.VMEM((SUBS * LEV * 3 * FR, 128), F32),
            pltpu.VMEM((SUBS * LEV * 3 * FR, 128), F32),
            pltpu.VMEM((SUBS * (LEV + 1) * 3 * FR, 128), F32),
            pltpu.VMEM((NF * 2 * FR, 128), F32),
            pltpu.VMEM((NF * FR, 128), F32),
            pltpu.VMEM((96, 128), F32),
            pltpu.VMEM((n_main, 128), F32),
            pltpu.VMEM((n_side, 128), F32),
            pltpu.VMEM((n_main, 128), F32),
            pltpu.VMEM((n_side, 128), F32),
            pltpu.VMEM((2, PITCH * CY, 128), F32),
            pltpu.VMEM((128 * CY, 256), BF16),
            pltpu.VMEM((256, 2048), BF16),
            pltpu.VMEM((8 * NTR, 24 * NTR), BF16),
            pltpu.VMEM((NTR, LEV, CY, CX), F32),
            pltpu.SemaphoreType.DMA((2,)),
        ]
        + [
            pltpu.VMEM((24 * NTR, 384), BF16),
            pltpu.VMEM((8 * NTR, 384), F32),
            pltpu.VMEM((3 * 8 * 8, 128), F32),
        ]
        * 2,
        limit=20,
        in_specs=[vmem] * 10 + [hbm, vmem],
        out_specs=(hbm, vmem),
        flops=BUSY,
    )(tracers, ocean_mask, below, above, from_west, from_east, bio_rates, lines, f_below, f_above, pltpu.with_memory_space_constraint(hot, pltpu.HBM), yrow)

    agent_state = call(
        agents_kernel,
        full(16, 64, 128),
        [pltpu.VMEM((64, 384), BF16)],
        in_specs=[vmem] * 4 + [pl.BlockSpec(memory_space=pltpu.SMEM)],
    )(received, picked, trait_weights, env_weights, agent_counts)
    return (tracers_out, agent_state[None, None])


def solution(mesh):
    placed = (
        P(None, None, "lat", "lon"),
        P(("lat", "lon"), None, None),
        P(("lat", "lon"), None),
        P("lat", "lon"),
        P(),
        P("lat", "lon", None, None, None),
        P("lat", None, None, None),
        P("lat", None, None),
        P(),
        P(),
    )
    return jax.shard_map(
        shards,
        mesh=mesh,
        in_specs=placed,
        out_specs=(P(None, None, "lat", "lon"), P("lat", "lon", None, None, None)),
        check_vma=False,
    )
```

```python
import jax
import jax.numpy as jnp
from jax import lax
from jax.experimental import pallas as pl
from jax.experimental.pallas import tpu as pltpu
from jax.sharding import PartitionSpec as P

NTR = 10
LEV = 6
SUBS = 3
CY = 16
CX = 256
BIO_STEP = 0.2
PRECISE = lax.Precision.HIGHEST

F32 = jnp.float32
BF16 = jnp.bfloat16

LINES = 14
PITCH = 65
BUSY = 10**12
FR = 26
NF = NTR * LEV + 1


def call(kernel, outs, scratch=(), limit=8, flops=0, in_specs=None, out_specs=None):
    return pl.pallas_call(
        kernel,
        out_shape=outs,
        scratch_shapes=list(scratch),
        **({"in_specs": in_specs} if in_specs else {}),
        **({"out_specs": out_specs} if out_specs else {}),
        compiler_params=pltpu.CompilerParams(vmem_limit_bytes=limit * 1024 * 1024),
        cost_estimate=pl.CostEstimate(flops=flops, bytes_accessed=0, transcendentals=0),
    )


def full(*shape, dtype=F32):
    return jax.ShapeDtypeStruct(shape, dtype)


def three_parts(x):
    hi = x.astype(BF16)
    rest = x - hi.astype(F32)
    mid = rest.astype(BF16)
    lo = (rest - mid.astype(F32)).astype(BF16)
    return hi, mid, lo


def dot(a, b):
    return jnp.dot(a, b, preferred_element_type=F32)


def lane_iota(rows=8):
    return lax.broadcasted_iota(jnp.int32, (rows, 128), 1)


def sort_bands_kernel(bands_hbm_ref, tiles_hbm_ref, out_ref, xs_ref, ends_ref, tiles_ref, in_sems):
    reader = lax.axis_index("lat") * 16 + lax.axis_index("lon")
    odd = lax.rem(reader, 2)
    top = pl.multiple_of(8 + 64 * odd, 8)
    chunk = 432
    copies = [
        pltpu.make_async_copy(
            bands_hbm_ref.at[0, pl.ds(chunk * k, chunk)],
            xs_ref.at[pl.ds(pl.multiple_of(top + chunk * k, 8), chunk)],
            in_sems.at[k],
        )
        for k in range(4)
    ]
    tiles_copy = pltpu.make_async_copy(tiles_hbm_ref, tiles_ref, in_sems.at[4])
    tiles_copy.start()
    for copy in copies:
        copy.start()
    spare = pl.multiple_of(64 * (1 - odd), 8)
    xs_ref[0:8, :] = jnp.zeros((8, 128), F32)
    xs_ref[8 + LINES * 128 : 16 + LINES * 128, :] = jnp.zeros((8, 128), F32)
    xs_ref[pl.ds(pl.multiple_of(8 + 27 * 64 * (1 - odd), 8), 64), :] = jnp.zeros((64, 128), F32)
    ends_ref[...] = jnp.zeros(ends_ref.shape, F32)

    tiles_copy.wait()
    tiles = tiles_ref[0:1, :]
    me = lax.broadcasted_iota(jnp.int32, (128, 128), 0)
    west = (me & -16) | ((me - 1) & 15)
    east = (me & -16) | ((me + 1) & 15)
    own_hot, west_hot, east_hot = [
        (tiles == t).astype(F32).astype(BF16) for t in (me, west, east)
    ]

    def pick(hot, k_rows):
        a, b, c = [
            lax.dot_general(hot, part, (((1,), (1,)), ((), ())), preferred_element_type=F32)
            for part in k_rows
        ]
        return (c + b) + a

    def sort_block(block, halo):
        lo = 8 + 256 * block
        t = pick(own_hot, three_parts(xs_ref[lo : lo + 256, :]))
        for k in range(2):
            line = 2 * block + k
            part = t[:, k * 128 : k * 128 + 128]
            if line == 0:
                part = part + jnp.where(odd == 1, halo, 0.0)
            if line == LINES - 1:
                part = part + jnp.where(odd == 1, 0.0, halo)
            for g in range(16):
                out_ref[pl.ds(8 * LINES * g + line, 8, stride=LINES), :] = part[8 * g : 8 * g + 8]

    arrived = 0
    for block in range(1, LINES // 2 - 1):
        while arrived * chunk < 256 * block + 256:
            copies[arrived].wait()
            arrived += 1
        sort_block(block, None)
    case = lax.rem(reader, 4)
    first = lax.div(case + 1, 2)
    for j in range(7):
        at = 8 + 128 * first + 256 * j
        ends_ref[pl.ds(spare + 8 * j + 5, 3), :] = xs_ref[pl.ds(at - 3, 3), :]
        ends_ref[pl.ds(128 + spare + 8 * j, 3), :] = xs_ref[pl.ds(at, 3), :]
    parts = three_parts(ends_ref[...])
    halo = pick(west_hot, [p[:128] for p in parts]) + pick(east_hot, [p[128:] for p in parts])
    sort_block(0, halo)
    sort_block(LINES // 2 - 1, halo)


def north_rows():
    for s in range(2 + 1):
        for f in range(3):
            n = (2, 3, 2)[f] - s
            for l in range(LEV - (f == 2)):
                if n > 0:
                    yield s, f, l, n


def south_rows():
    for s in range(2):
        for f in range(3):
            for l in range(LEV - (f == 2)):
                yield s, f, l, 2 - s


NORTH = 3 * sum(r[3] for r in north_rows())
SOUTH = 3 * sum(r[3] for r in south_rows())


def unpack(lines_ref, flat_ref, edge_ref):
    lane = lane_iota()
    for p in range(64):
        a, b = 27 * p, 28 * p
        for to, frm in ((0, 0), (5, 5), (14, 15), (19, 20)):
            flat_ref[a + to : a + to + 8, :] = lines_ref[b + frm : b + frm + 8, :]
        flat_ref[a + 13 : a + 14, :] = jnp.where(
            lane[:1] < 64, lines_ref[b + 13 : b + 14, :], lines_ref[b + 14 : b + 15, :]
        )
    for gg in range(4):
        spare = [
            lines_ref[pl.ds(448 * gg + off, 8, stride=56), :] for off in (13, 14, 41, 42)
        ]
        for n in range(27):
            i, j = divmod(n, 7)
            right = pltpu.roll(spare[i], (128 - ((64, 0)[i % 2] + 8 * j)) % 128, 1)
            i, j = divmod(n + 1, 7)
            left = pltpu.roll(spare[i], (128 - ((64, 0)[i % 2] + 8 * j + 8)) % 128, 1)
            edge_ref[pl.ds(216 * gg + n, 8, stride=27), :] = jnp.where(lane < 64, right, left)


def edge_rows_kernel(lines_ref, west_ref, east_ref, north_ref, south_ref, flat_ref, edge_ref):
    unpack(lines_ref, flat_ref, edge_ref)
    at = 0
    for s, f, l, n in north_rows():
        q = (s * 3 + f) * LEV + l
        for h in range(2):
            north_ref[at : at + n, :] = flat_ref[pl.ds(32 * q + 2 * (CY - n) + h, n, stride=2), :]
            at += n
        north_ref[at : at + n, :] = edge_ref[16 * q + CY - n : 16 * q + CY, :]
        at += n
    at = 0
    for s, f, l, n in south_rows():
        q = (s * 3 + f) * LEV + l
        for h in range(2):
            south_ref[at : at + n, :] = flat_ref[pl.ds(32 * q + h, n, stride=2), :]
            at += n
        south_ref[at : at + n, :] = edge_ref[16 * q : 16 * q + n, :]
        at += n
    k = 0
    for ref in (west_ref, east_ref):
        for half in range(2):
            north_ref[NORTH + k : NORTH + k + 3, :] = ref[16 * half + 13 : 16 * half + 16, :]
            south_ref[SOUTH + k : SOUTH + k + 3, :] = ref[16 * half : 16 * half + 3, :]
            k += 3


def field(tracers_ref, ocean_ref, f, rows, cols):
    if f < NTR * LEV:
        l, c = divmod(f, NTR)
        return tracers_ref[c, l, rows, cols]
    return ocean_ref[rows, cols].astype(F32)


def ends_kernel(tracers_ref, ocean_ref, north_ref, south_ref, east_ref, west_ref):
    lane = lane_iota()
    for f in range(NF):
        for h in range(2):
            cols = slice(128 * h, 128 * h + 128)
            at = (f * 2 + h) * 3
            north_ref[at : at + 3, :] = field(tracers_ref, ocean_ref, f, slice(CY - 3, CY), cols)
            south_ref[at : at + 3, :] = field(tracers_ref, ocean_ref, f, slice(0, 3), cols)
    for half in range(2):
        for g in range(2):
            rows = slice(8 * g, 8 * g + 8)
            east = jnp.zeros((8, 128), F32)
            west = jnp.zeros((8, 128), F32)
            for f in range(32 * half, min(32 * half + 32, NF)):
                m = 4 * (f % 32)
                use = (lane >= m) & (lane < m + 3)
                last = field(tracers_ref, ocean_ref, f, rows, slice(128, 256))
                first = field(tracers_ref, ocean_ref, f, rows, slice(0, 128))
                east = jnp.where(use, pltpu.roll(last, (m + 3) % 128, 1), east)
                west = jnp.where(use, pltpu.roll(first, m, 1) if m else first, west)
            to = 16 * half + 8 * g
            east_ref[to : to + 8, :] = east
            west_ref[to : to + 8, :] = west


def fill_frames(
    tracers_ref, ocean_ref, below_ref, above_ref, west_ref, east_ref, f_below_ref, f_above_ref,
    main_ref, side_ref, ends_ref,
):
    zero = jnp.zeros((4, 128), F32)
    for f in range(NF):
        for h in range(2):
            cols = slice(128 * h, 128 * h + 128)
            at, frm = (f * 2 + h) * FR, (f * 2 + h) * 3
            main_ref[at : at + 3, :] = below_ref[frm : frm + 3, :]
            for g in range(2):
                main_ref[at + 3 + 8 * g : at + 11 + 8 * g, :] = field(
                    tracers_ref, ocean_ref, f, slice(8 * g, 8 * g + 8), cols
                )
            main_ref[at + 19 : at + 22, :] = above_ref[frm : frm + 3, :]
            main_ref[at + 22 : at + 26, :] = zero
    for k in range(4):
        ref, half, to = (west_ref, east_ref)[k // 2], k % 2, 24 * k
        ends_ref[to : to + 3, :] = f_below_ref[NORTH + 3 * k : NORTH + 3 * k + 3, :]
        ends_ref[to + 3 : to + 11, :] = ref[16 * half : 16 * half + 8, :]
        ends_ref[to + 11 : to + 19, :] = ref[16 * half + 8 : 16 * half + 16, :]
        ends_ref[to + 19 : to + 22, :] = f_above_ref[SOUTH + 3 * k : SOUTH + 3 * k + 3, :]
        ends_ref[to + 22 : to + 24, :] = zero[:2]
    lane = lane_iota()
    for f in range(NF):
        m = 4 * (f % 32)
        frm = 24 * (f // 32)
        for g in range(3):
            right = ends_ref[48 + frm + 8 * g : 56 + frm + 8 * g, :]
            if m:
                right = pltpu.roll(right, 128 - m, 1)
            left = pltpu.roll(ends_ref[frm + 8 * g : frm + 8 * g + 8, :], 125 - m, 1)
            side_ref[f * FR + 8 * g : f * FR + 8 * g + 8, :] = jnp.where(lane < 64, right, left)
        side_ref[f * FR + 24 : f * FR + 26, :] = zero[:2]


def shift_east(tiles, lane):
    moved = [pltpu.roll(t, 127, 1) for t in tiles]
    n = len(tiles)
    return [jnp.where(lane == 127, moved[(h + 1) % n], moved[h]) for h in range(n)]


def shift_west(tiles, lane):
    moved = [pltpu.roll(t, 1, 1) for t in tiles]
    n = len(tiles)
    return [jnp.where(lane == 0, moved[(h - 1) % n], moved[h]) for h in range(n)]


def transport_kernel(
    tracers_ref,
    ocean_ref,
    t_below_ref,
    t_above_ref,
    west_ref,
    east_ref,
    bio_ref,
    lines_ref,
    below_ref,
    above_ref,
    hot_hbm_ref,
    yrow_ref,
    out_hbm_ref,
    picked_ref,
    flat_ref,
    edge_ref,
    u_ref,
    v_ref,
    k_ref,
    main_ref,
    side_ref,
    ends_ref,
    main1_ref,
    side1_ref,
    main2_ref,
    side2_ref,
    env_ref,
    lhs_ref,
    hot_ref,
    rates_ref,
    out_ref,
    sems,
    *work_refs,
):
    hot_copy = pltpu.make_async_copy(hot_hbm_ref, hot_ref, sems.at[0])
    hot_copy.start()

    shape = (8 * NTR, NTR)
    spread = lax.broadcasted_iota(jnp.int32, shape, 0) // 8 == lax.broadcasted_iota(jnp.int32, shape, 1)
    spread = spread.astype(F32)
    wide = jnp.dot(spread, BIO_STEP * bio_ref[...], preferred_element_type=F32, precision=PRECISE)
    wide = lax.dot_general(
        wide, spread, (((1,), (1,)), ((), ())), preferred_element_type=F32, precision=PRECISE
    )
    row = lax.broadcasted_iota(jnp.int32, wide.shape, 0)
    column = lax.broadcasted_iota(jnp.int32, wide.shape, 1)
    wide = jnp.where((row & 7) == (column & 7), wide, 0.0)
    hi = wide.astype(BF16)
    lo = (wide - hi.astype(F32)).astype(BF16)
    rates_ref[...] = jnp.concatenate([hi, hi, lo], axis=1)
    fill_frames(
        tracers_ref, ocean_ref, t_below_ref, t_above_ref, west_ref, east_ref, below_ref, above_ref,
        main_ref, side_ref, ends_ref,
    )
    lane = lane_iota()
    unpack(lines_ref, flat_ref, edge_ref)

    below, above = {}, {}
    at = 0
    for s, f, l, n in north_rows():
        below[s, f, l] = (at, n)
        at += 3 * n
    at = 0
    for s, f, l, n in south_rows():
        above[s, f, l] = (at, n)
        at += 3 * n
    for s in range(SUBS):
        for f in range(3):
            ref = (u_ref, v_ref, k_ref)[f]
            for l in range(LEV - (f == 2)):
                q = (s * 3 + f) * LEV + l
                k = s * LEV + l if f < 2 else s * (LEV + 1) + l + 1
                for h in range(3):
                    to = (k * 3 + h) * FR
                    if s == 0:
                        ref[to + 19 : to + 26, :] = jnp.zeros((7, 128), F32)
                    for g in range(2):
                        if h < 2:
                            part = flat_ref[pl.ds(32 * q + 16 * g + h, 8, stride=2), :]
                        else:
                            part = edge_ref[16 * q + 8 * g : 16 * q + 8 * g + 8, :]
                        ref[to + 3 + 8 * g : to + 11 + 8 * g, :] = part
                    if (s, f, l) in below:
                        frm, n = below[s, f, l]
                        ref[to + 3 - n : to + 3, :] = below_ref[frm + h * n : frm + h * n + n, :]
                    if (s, f, l) in above:
                        frm, n = above[s, f, l]
                        ref[to + 19 : to + 19 + n, :] = above_ref[frm + h * n : frm + h * n + n, :]
        for k in (s * (LEV + 1), s * (LEV + 1) + LEV):
            for r in range(0, 3 * FR, 6):
                k_ref[k * 3 * FR + r : k * 3 * FR + r + 6, :] = jnp.zeros((6, 128), F32)

    def substep(s, src, dst):
        start = 1 if s < 2 else 3
        groups = 3 if s < 2 else 2
        width = 3 if s < 2 else 2
        smain, sside = src

        def place(t):
            l = lax.div(t, groups)
            g = lax.rem(t, groups)
            return l, g, start + 8 * g

        def readers(row):
            def frame(f, h, off=0):
                if h < 2:
                    return smain[pl.ds((f * 2 + h) * FR + row + off, 8), :]
                return sside[pl.ds(f * FR + row + off, 8), :]

            def forcing(ref, k, h, off=0):
                return ref[pl.ds((k * 3 + h) * FR + row + off, 8), :]

            def ocean(h, off=0):
                f = NTR * LEV
                if h < 2:
                    return main_ref[pl.ds((f * 2 + h) * FR + row + off, 8), :]
                return side_ref[pl.ds(f * FR + row + off, 8), :]

            return frame, forcing, ocean

        def prepare(t, slot):
            split_ref, grown_ref, coef_ref = work_refs[3 * slot : 3 * slot + 3]
            l, g, row = place(t)
            frame, forcing, ocean = readers(row)
            for h in range(width):
                x = jnp.concatenate([frame(l * NTR + c, h) for c in range(NTR)], axis=0)
                hi = x.astype(BF16)
                lo = (x - hi.astype(F32)).astype(BF16)
                cols = slice(128 * h, 128 * h + 128)
                split_ref[0:80, cols] = hi
                split_ref[80:160, cols] = lo
                split_ref[160:240, cols] = hi
            grown_ref[:, : 128 * width] = dot(rates_ref[...], split_ref[:, : 128 * width])

            o = [ocean(h) for h in range(3)]
            u = [forcing(u_ref, s * LEV + l, h) for h in range(3)]
            open_east = [a * b for a, b in zip(o, shift_east(o, lane))]
            up = [w * jnp.maximum(x, 0.0) for w, x in zip(open_east, u)]
            um = [w * jnp.minimum(x, 0.0) for w, x in zip(open_east, u)]
            up_w, um_w = shift_west(up, lane), shift_west(um, lane)
            for h in range(width):
                v = forcing(v_ref, s * LEV + l, h)
                v_s = forcing(v_ref, s * LEV + l, h, -1)
                open_n, open_s = o[h] * ocean(h, 1), o[h] * ocean(h, -1)
                vp, vm = open_n * jnp.maximum(v, 0.0), open_n * jnp.minimum(v, 0.0)
                vp_s, vm_s = open_s * jnp.maximum(v_s, 0.0), open_s * jnp.minimum(v_s, 0.0)
                k_up = o[h] * forcing(k_ref, s * (LEV + 1) + l + 1, h)
                k_dn = o[h] * forcing(k_ref, s * (LEV + 1) + l, h)
                own = (um_w[h] - up[h]) + (vm_s - vp) - (k_up + k_dn)
                own = own + 1.0
                values = (own, -um[h], up_w[h], -vm, vp_s, k_up, k_dn, o[h])
                for i, value in enumerate(values):
                    coef_ref[(h * 8 + i) * 8 : (h * 8 + i) * 8 + 8, :] = value

        def transport(t, slot):
            grown_ref, coef_ref = work_refs[3 * slot + 1 : 3 * slot + 3]
            l, g, row = place(t)
            frame = readers(row)[0]

            l_up, l_dn = jnp.minimum(l + 1, LEV - 1), jnp.maximum(l - 1, 0)
            coefs = [
                [coef_ref[(h * 8 + i) * 8 : (h * 8 + i) * 8 + 8, :] for i in range(8)]
                for h in range(width)
            ]
            for a in range(NTR):
                f = l * NTR + a
                cell = [frame(f, h) for h in range(3)]
                east, west = shift_east(cell, lane), shift_west(cell, lane)
                for h in range(width):
                    own, k_e, k_w, k_n, k_s, k_up, k_dn, water = coefs[h]
                    value = (own * cell[h] + k_e * east[h]) + (k_w * west[h] + k_n * frame(f, h, 1))
                    value = value + (k_s * frame(f, h, -1) + k_up * frame(l_up * NTR + a, h))
                    value = value + k_dn * frame(l_dn * NTR + a, h)
                    value = value + water * grown_ref[8 * a : 8 * a + 8, 128 * h : 128 * h + 128]
                    if s == 2:
                        rows = pl.ds(pl.multiple_of(8 * g, 8), 8)
                        out_ref[a, l, rows, 128 * h : 128 * h + 128] = value
                        env_ref[h, pl.ds(8 * PITCH * g + a * LEV + l, 8, stride=PITCH), :] = value
                    elif h < 2:
                        dst[0][pl.ds((f * 2 + h) * FR + row, 8), :] = value
                    else:
                        dst[1][pl.ds(f * FR + row, 8), :] = value

        count = groups * LEV

        def body(k, _):
            prepare(2 * k + 1, 1)
            transport(2 * k, 0)
            prepare(jnp.minimum(2 * k + 2, count - 1), 0)
            transport(2 * k + 1, 1)
            return 0

        prepare(0, 0)
        lax.fori_loop(0, count // 2, body, 0)

    substep(0, (main_ref, side_ref), (main1_ref, side1_ref))
    substep(1, (main1_ref, side1_ref), (main2_ref, side2_ref))
    substep(2, (main2_ref, side2_ref), None)

    out_copy = pltpu.make_async_copy(out_ref, out_hbm_ref, sems.at[1])
    out_copy.start()

    for y in range(CY):
        for h in range(2):
            env_ref[h, PITCH * y + NTR * LEV : PITCH * y + 64, :] = jnp.zeros((4, 128), F32)
            x = env_ref[h, PITCH * y : PITCH * y + 64, :]
            hi = x.astype(BF16)
            lo = (x - hi.astype(F32)).astype(BF16)
            lhs_ref[128 * y : 128 * y + 64, 128 * h : 128 * h + 128] = hi
            lhs_ref[128 * y + 64 : 128 * y + 128, 128 * h : 128 * h + 128] = lo

    hot_copy.wait()

    def slots(n, _):
        cols = pl.ds(pl.multiple_of(256 * n, 256), 256)
        found = dot(lhs_ref[...], hot_ref[:, cols])
        row = yrow_ref[0:1, cols]
        total = jnp.where(row == 0, found[:64] + found[64:128], 0.0)
        for y in range(1, CY):
            here = found[128 * y : 128 * y + 64] + found[128 * y + 64 : 128 * y + 128]
            total = total + jnp.where(row == y, here, 0.0)
        hi = total.astype(BF16)
        picked_ref[0:64, cols] = hi
        picked_ref[64:128, cols] = (total - hi.astype(F32)).astype(BF16)
        return 0

    lax.fori_loop(0, 8, slots, 0)
    out_copy.wait()


def slots_kernel(cells_ref, hot_ref, yrow_ref):
    own = lax.axis_index("lon")
    column = lax.broadcasted_iota(jnp.int32, (256, 128), 0)
    for n in range(16):
        cell = cells_ref[0, n, pl.ds(own, 1), :]
        hot_ref[:, 128 * n : 128 * n + 128] = ((cell & 255) == column).astype(F32).astype(BF16)
        yrow_ref[:, 128 * n : 128 * n + 128] = lax.shift_right_logical(cell, 8)


def agents_kernel(
    traits_ref, picked_ref, tw_ref, ew_ref, counts_ref, out_hbm_ref, out_ref, weights_ref, sems
):
    first, second = [
        pltpu.make_async_copy(out_ref.at[here], out_hbm_ref.at[here], sems.at[k])
        for k, here in enumerate((pl.ds(0, 8), pl.ds(8, 8)))
    ]
    own = lax.axis_index("lon")
    ew = jnp.concatenate([ew_ref[...], jnp.zeros((4, 64), F32)], axis=0)
    for k, w in enumerate((tw_ref[...], ew)):
        w = w.T
        hi = w.astype(BF16)
        lo = (w - hi.astype(F32)).astype(BF16)
        for i, part in enumerate((hi, hi, lo)):
            weights_ref[:, (3 * k + i) * 64 : (3 * k + i) * 64 + 64] = part
    slot = lax.broadcasted_iota(jnp.int32, (64, 128), 1)
    for n in range(0, 16, 2):
        x = jnp.concatenate([traits_ref[n], traits_ref[n + 1]], axis=1)
        hi = x.astype(BF16)
        lo = (x - hi.astype(F32)).astype(BF16)
        picked = picked_ref[:, 128 * n : 128 * n + 256]
        rhs = jnp.concatenate([hi, lo, hi, picked, picked[:64]], axis=0)
        new = x + jnp.tanh(dot(weights_ref[...], rhs))
        for k in range(2):
            live = slot < counts_ref[0, n + k, own]
            out_ref[n + k] = jnp.where(live, new[:, 128 * k : 128 * k + 128], 0.0)
        if n == 6:
            first.start()
    second.start()
    first.wait()
    second.wait()


def shards(
    tracers,
    forcing_groups,
    group_tiles,
    ocean_mask,
    bio_rates,
    agent_traits,
    agent_cells,
    agent_counts,
    trait_weights,
    env_weights,
):
    north = [(i, i + 1) for i in range(7)]
    south = [(i + 1, i) for i in range(7)]
    east = [(i, (i + 1) % 16) for i in range(16)]
    west = [((i + 1) % 16, i) for i in range(16)]

    vmem = pl.BlockSpec(memory_space=pltpu.VMEM)
    hbm = pl.BlockSpec(memory_space=pltpu.HBM)

    bands = jnp.swapaxes(forcing_groups, 1, 2)
    lines = call(
        sort_bands_kernel,
        pltpu.VMEM((128 * LINES, 128), F32),
        [
            pltpu.VMEM((16 + LINES * 128, 128), F32),
            pltpu.VMEM((256, 128), F32),
            pltpu.VMEM((1, 128), jnp.int32),
            pltpu.SemaphoreType.DMA((5,)),
        ],
        in_specs=[hbm, hbm],
    )(
        pltpu.with_memory_space_constraint(bands, pltpu.HBM),
        pltpu.with_memory_space_constraint(group_tiles, pltpu.HBM),
    )
    lines = lines.reshape(128, 1, LINES * 128)
    lines = lax.all_to_all(lines, ("lat", "lon"), split_axis=0, concat_axis=0, tiled=True)
    lines = lines.reshape(128 * LINES, 128)

    n_rows, n_cols = full(NF * 6, 128), full(32, 128)
    to_north, to_south, to_east, to_west = call(ends_kernel, (n_rows, n_rows, n_cols, n_cols))(
        tracers, ocean_mask
    )
    below = lax.ppermute(to_north, "lat", north)
    above = lax.ppermute(to_south, "lat", south)
    from_west = lax.ppermute(to_east, "lon", east)
    from_east = lax.ppermute(to_west, "lon", west)
    hot, yrow = call(
        slots_kernel, (full(256, 2048, dtype=BF16), full(1, 2048, dtype=jnp.int32))
    )(agent_cells)
    lines, below, above, from_west, from_east, hot, yrow = lax.optimization_barrier(
        (lines, below, above, from_west, from_east, hot, yrow)
    )
    f_north, f_south = call(
        edge_rows_kernel,
        (full(NORTH + 12, 128), full(SOUTH + 12, 128)),
        [pltpu.VMEM((1728, 128), F32), pltpu.VMEM((864, 128), F32)],
    )(lines, from_west, from_east)
    f_below = lax.ppermute(f_north, "lat", north)
    f_above = lax.ppermute(f_south, "lat", south)
    traits, _ = lax.optimization_barrier((agent_traits[0, 0], f_north))
    received = lax.all_to_all(traits, "lon", split_axis=0, concat_axis=0, tiled=True)

    n_main, n_side = NTR * LEV * 2 * FR, NTR * LEV * FR
    tracers_out, picked = call(
        transport_kernel,
        (pltpu.HBM((NTR, LEV, CY, CX), F32), full(128, 2048, dtype=BF16)),
        [
            pltpu.VMEM((1728, 128), F32),
            pltpu.VMEM((864, 128), F32),
            pltpu.VMEM((SUBS * LEV * 3 * FR, 128), F32),
            pltpu.VMEM((SUBS * LEV * 3 * FR, 128), F32),
            pltpu.VMEM((SUBS * (LEV + 1) * 3 * FR, 128), F32),
            pltpu.VMEM((NF * 2 * FR, 128), F32),
            pltpu.VMEM((NF * FR, 128), F32),
            pltpu.VMEM((96, 128), F32),
            pltpu.VMEM((n_main, 128), F32),
            pltpu.VMEM((n_side, 128), F32),
            pltpu.VMEM((n_main, 128), F32),
            pltpu.VMEM((n_side, 128), F32),
            pltpu.VMEM((2, PITCH * CY, 128), F32),
            pltpu.VMEM((128 * CY, 256), BF16),
            pltpu.VMEM((256, 2048), BF16),
            pltpu.VMEM((8 * NTR, 24 * NTR), BF16),
            pltpu.VMEM((NTR, LEV, CY, CX), F32),
            pltpu.SemaphoreType.DMA((2,)),
        ]
        + [
            pltpu.VMEM((24 * NTR, 384), BF16),
            pltpu.VMEM((8 * NTR, 384), F32),
            pltpu.VMEM((3 * 8 * 8, 128), F32),
        ]
        * 2,
        limit=20,
        in_specs=[vmem] * 10 + [hbm, vmem],
        out_specs=(hbm, vmem),
        flops=BUSY,
    )(tracers, ocean_mask, below, above, from_west, from_east, bio_rates, lines, f_below, f_above, pltpu.with_memory_space_constraint(hot, pltpu.HBM), yrow)

    agent_state = call(
        agents_kernel,
        pltpu.HBM((16, 64, 128), F32),
        [
            pltpu.VMEM((16, 64, 128), F32),
            pltpu.VMEM((64, 384), BF16),
            pltpu.SemaphoreType.DMA((2,)),
        ],
        in_specs=[vmem] * 4 + [pl.BlockSpec(memory_space=pltpu.SMEM)],
        out_specs=hbm,
    )(received, picked, trait_weights, env_weights, agent_counts)
    return (tracers_out, agent_state[None, None])


def solution(mesh):
    placed = (
        P(None, None, "lat", "lon"),
        P(("lat", "lon"), None, None),
        P(("lat", "lon"), None),
        P("lat", "lon"),
        P(),
        P("lat", "lon", None, None, None),
        P("lat", None, None, None),
        P("lat", None, None),
        P(),
        P(),
    )
    return jax.shard_map(
        shards,
        mesh=mesh,
        in_specs=placed,
        out_specs=(P(None, None, "lat", "lon"), P("lat", "lon", None, None, None)),
        check_vma=False,
    )
```
